32 devices in a mesh: groups: 2 (over x), blk: 16 (over z, y, core).
Axes of the slice: x: 2, y: 2, z: 4, core: 2. Of those that a mesh axis runs over, the one named last changes fastest.
Arguments:
- mesh_in: bfloat16 [8192, 512], P(('groups', 'blk')), parts along dimension 0, may hold values from -40 to 40
- grid_in: bfloat16 [4096, 512], P(('groups', 'blk')), parts along dimension 0, may hold values from -6 to 6
- cotangent: bfloat16 [4096, 512], P(('groups', 'blk')), parts along dimension 0, may hold values from -6 to 6
- w_send: bfloat16 [512, 512], replicated, may hold values from -0.25 to 0.25
- w_self: bfloat16 [512, 512], replicated, may hold values from -0.25 to 0.25
- w_out: bfloat16 [512, 512], replicated, may hold values from -0.25 to 0.25
- w_src: bfloat16 [512, 512], replicated, may hold values from -0.25 to 0.25
- w_dst: bfloat16 [512, 512], replicated, may hold values from -0.25 to 0.25
- w_dec: bfloat16 [512, 512], replicated, may hold values from -0.25 to 0.25
- adj_blocks: bfloat16 [32, 4, 128, 128], P('blk'), may hold values from -0.25 to 0.25
- adj_index: int32 [32, 4], replicated, may hold values from 0 to 31, as said below
- src_rows: int32 [16, 5, 64], P('blk'), may hold values from 0 to 255
- dst_rows: int32 [16, 5, 64], P('blk'), may hold values from 0 to 127
- counts: int32 [16, 5], P('blk'), may hold values from 1 to 64, as said below
Outputs:
- grid_out: bfloat16 [4096, 512], P(('groups', 'blk')), parts along dimension 0
- grad_grid: bfloat16 [4096, 512], P(('groups', 'blk')), parts along dimension 0
- grad_mesh: bfloat16 [8192, 512], P(('groups', 'blk')), parts along dimension 0
The draws below stay inside these ranges and needn't reach their ends.
There are 2 independent parts, one for each index of `groups`. The reference program is written for one: setup_inputs(seed, part) draws one part's arguments, and reference() takes and returns one part's arrays. A program takes and returns all parts, laid end to end along the dimension named above; an argument that names none is the same for every part. Nothing has to cross between parts.
Inputs may be any that keep to these rules, and one draw needn't show every extreme that they name: `adj_index`: column 0 names the block itself; every entry names a block on a device at cycle distance at most 2 (device indices wrap around), and every row has one entry at distance 2 on each side. `counts`: some destination has all 64 slots live from each of its 5 owners, and some owner has all 64 slots live to each of its destinations.
All inputs are finite; a program needn't handle non-finite values.
Results may differ from the reference program's by a relative error of at most 0.0085.
Values may be sent and summed in bfloat16 or wider, within the bound.
A program may use at most 64 MiB of HBM per device.

```python
import math
import jax
import jax.numpy as jnp
from jax import lax

D = 512
BPD = 2
GRID_DEV = 128
K = 4
REACH = 2
OWNERS = 5
MESH_DEV = 256
SLOTS = 64
MESH = 4096
GRID = 2048
NBLOCKS = 32
N_BLK = 16


def draw_mesh_in(key, part):
    key = jax.random.fold_in(key, 5)
    first, second, third = jax.random.split(key, 3)
    rows = jnp.exp(jax.random.uniform(first, (MESH, 1), jnp.float32) * math.log(10.0))
    cols = jnp.exp(jax.random.uniform(second, (1, D), jnp.float32) * math.log(10.0))
    base = jax.random.truncated_normal(third, -4.0, 4.0, (MESH, D), jnp.float32)
    return (base * rows * cols / 10.0).astype(jnp.bfloat16)


def draw_adj_index(key, part):
    key = jax.random.fold_in(key, 11)
    first, second = jax.random.split(key, 2)
    nblk = BPD * N_BLK
    block = jnp.arange(nblk, dtype=jnp.int32)
    device = block // BPD
    fixed = jnp.stack([jnp.zeros((nblk,), jnp.int32), jnp.full((nblk,), -REACH, jnp.int32), jnp.full((nblk,), REACH, jnp.int32)], axis=1)
    others = jax.random.randint(first, (nblk, K - 3), -REACH, REACH + 1, dtype=jnp.int32)
    offsets = jnp.concatenate([fixed, others], axis=1)
    local = jax.random.randint(second, (nblk, K), 0, BPD, dtype=jnp.int32)
    local = local.at[:, 0].set(block % BPD)
    return (device[:, None] + offsets + N_BLK) % N_BLK * BPD + local


def draw_counts(key, part):
    key = jax.random.fold_in(key, 17)
    first, second, third, fourth = jax.random.split(key, 4)
    places = 2 * REACH + 1
    low = max(1, SLOTS // 4)
    busy = jax.random.randint(first, (N_BLK,), 1, 4, dtype=jnp.int32)
    base = jax.random.randint(second, (N_BLK, places), low, SLOTS // 2 + 1, dtype=jnp.int32)
    dest = jnp.arange(N_BLK, dtype=jnp.int32)[:, None]
    place = jnp.arange(places, dtype=jnp.int32)[None, :]
    owner = (dest + place - REACH + N_BLK) % N_BLK
    filled = jnp.minimum(base * busy[owner], SLOTS)
    full_row = jax.random.randint(third, (), 0, N_BLK, dtype=jnp.int32)
    full_owner = jax.random.randint(fourth, (), 0, N_BLK, dtype=jnp.int32)
    whole = (dest == full_row) | (owner == full_owner)
    return jnp.where(whole, SLOTS, filled).astype(jnp.int32)


def plant(drawn, own_key, low, largest):
    dims = drawn.shape
    spot = [jax.random.randint(jax.random.fold_in(own_key, axis), (), 0, dims[axis]) for axis in range(len(dims))]
    drawn = drawn.at[tuple(spot)].set(low)
    longest = dims.index(max(dims))
    spot[longest] = (spot[longest] + 1) % dims[longest]
    return drawn.at[tuple(spot)].set(largest)


def block_scale(stream_key, extent, pieces, low, top_value):
    level, own = 1.0, jax.random.fold_in(stream_key, 6)
    for dim, blocks in pieces:
        heights = jnp.exp(jax.random.uniform(jax.random.fold_in(own, dim), (blocks,), jnp.float32, low / len(pieces), top_value / len(pieces)))
        level = level * jnp.repeat(heights, extent[dim] // blocks).reshape([-1 if axis == dim else 1 for axis in range(len(extent))])
    return level


def scatter_about(own_key, shape, spread, reach, pieces=(), held_as=jnp.bfloat16):
    values = jax.random.normal(own_key, shape, jnp.float32) * spread
    if len(pieces) > 0:
        values = block_scale(own_key, shape, pieces, -0.22, 0.18) * values
    return jnp.clip(values, min=-reach, max=reach).astype(held_as)


def setup_inputs(seed: int = 0, part: int = 0) -> dict:
    arg_keys = jax.random.split(jax.random.key(seed), 15)
    part_keys = jax.random.split(jax.random.fold_in(arg_keys[14], part), 15)
    mesh_in = draw_mesh_in(jax.random.fold_in(jax.random.fold_in(arg_keys[14], part), 71), part)
    grid_in = scatter_about(part_keys[1], (GRID, D), 1.0, 6.0, ((0, 16),))
    cotangent = scatter_about(part_keys[2], (GRID, D), 1.0, 6.0, ((0, 16),))
    w_send = scatter_about(arg_keys[3], (D, D), D ** -0.5, 0.25)
    w_self = scatter_about(arg_keys[4], (D, D), D ** -0.5, 0.25)
    w_out = scatter_about(arg_keys[5], (D, D), D ** -0.5, 0.25)
    w_src = scatter_about(arg_keys[6], (D, D), D ** -0.5, 0.25)
    w_dst = scatter_about(arg_keys[7], (D, D), D ** -0.5, 0.25)
    w_dec = scatter_about(arg_keys[8], (D, D), D ** -0.5, 0.25)
    adj_blocks = scatter_about(arg_keys[9], (NBLOCKS, K, 128, 128), (128 * K) ** -0.5, 0.25, ((0, 16),))
    adj_index = draw_adj_index(jax.random.fold_in(arg_keys[14], 71), part)
    src_rows = plant(jax.random.randint(arg_keys[11], (N_BLK, OWNERS, SLOTS), 0, MESH_DEV), jax.random.fold_in(arg_keys[11], 1), 0, MESH_DEV - 1).astype(jnp.int32)
    dst_rows = plant(jax.random.randint(arg_keys[12], (N_BLK, OWNERS, SLOTS), 0, GRID_DEV), jax.random.fold_in(arg_keys[12], 1), 0, GRID_DEV - 1).astype(jnp.int32)
    counts = draw_counts(jax.random.fold_in(arg_keys[14], 71), part)
    return dict(mesh_in=mesh_in, grid_in=grid_in, cotangent=cotangent, w_send=w_send, w_self=w_self, w_out=w_out, w_src=w_src, w_dst=w_dst, w_dec=w_dec, adj_blocks=adj_blocks, adj_index=adj_index, src_rows=src_rows, dst_rows=dst_rows, counts=counts)


def silu_grad(value):
    sig = jax.nn.sigmoid(value)
    return sig * (1.0 + value * (1.0 - sig))

def reference(mesh_in, grid_in, cotangent, w_send, w_self, w_out, w_src, w_dst, w_dec, adj_blocks, adj_index, src_rows, dst_rows, counts):
    width = mesh_in.shape[1]
    nblk = adj_index.shape[0]
    h32 = mesh_in.astype(jnp.float32)
    scale = lax.rsqrt(lax.optimization_barrier(jnp.mean(h32 * h32, axis=-1, keepdims=True)) + 1e-05)
    normed = h32 * scale
    normed_b = normed.astype(jnp.bfloat16)
    sent = jnp.dot(normed_b, w_send, preferred_element_type=jnp.float32).astype(jnp.bfloat16)
    picked = sent.reshape(nblk, 128, width)[adj_index]
    agg = jnp.einsum('bkij,bkjd->bid', adj_blocks.astype(jnp.float32), picked.astype(jnp.float32)).reshape(-1, width)
    pre_act = jnp.dot(normed_b, w_self, preferred_element_type=jnp.float32) + agg
    act = jax.nn.silu(pre_act).astype(jnp.bfloat16)
    mesh_out = (h32 + jnp.dot(act, w_out, preferred_element_type=jnp.float32)).astype(jnp.bfloat16)
    src_proj = jnp.dot(mesh_out, w_src, preferred_element_type=jnp.float32).astype(jnp.bfloat16)
    dst_proj = jnp.dot(grid_in, w_dst, preferred_element_type=jnp.float32)
    slot_iota = jnp.arange(SLOTS, dtype=jnp.int32)
    places = jnp.arange(OWNERS, dtype=jnp.int32)
    dests = jnp.arange(N_BLK, dtype=jnp.int32)

    def one_dest(carry, dest):
        owner_ids = (dest + places - REACH + N_BLK) % N_BLK
        rows = owner_ids[:, None] * MESH_DEV + src_rows[dest]
        incoming = src_proj[rows.reshape(-1)]
        live_flat = (slot_iota[None, :] < counts[dest][:, None]).astype(jnp.float32).reshape(-1, 1)
        dst = dst_rows[dest].reshape(-1)
        start = (dest * GRID_DEV).astype(jnp.int32)
        dproj = lax.dynamic_slice_in_dim(dst_proj, start, GRID_DEV, 0)
        edge_pre = incoming.astype(jnp.float32) + dproj[dst]
        edge = jax.nn.silu(edge_pre) * live_flat
        grid_sum = jnp.zeros((GRID_DEV, width), jnp.float32).at[dst].add(edge).astype(jnp.bfloat16)
        g_here = lax.dynamic_slice_in_dim(grid_in, start, GRID_DEV, 0)
        out = (g_here.astype(jnp.float32) + jnp.dot(grid_sum, w_dec, preferred_element_type=jnp.float32)).astype(jnp.bfloat16)
        cot = lax.dynamic_slice_in_dim(cotangent, start, GRID_DEV, 0)
        d_sum = jnp.dot(cot, w_dec.T, preferred_element_type=jnp.float32).astype(jnp.bfloat16)
        d_edge = (d_sum[dst].astype(jnp.float32) * silu_grad(edge_pre) * live_flat).astype(jnp.bfloat16)
        d_dst = jnp.zeros((GRID_DEV, width), jnp.float32).at[dst].add(d_edge.astype(jnp.float32)).astype(jnp.bfloat16)
        grad_here = (cot.astype(jnp.float32) + jnp.dot(d_dst, w_dst.T, preferred_element_type=jnp.float32)).astype(jnp.bfloat16)
        carry = carry.at[rows.reshape(-1)].add(d_edge.astype(jnp.float32))
        return (carry, (out, grad_here))
    d_src, (outs, grads) = lax.scan(one_dest, jnp.zeros((MESH, width), jnp.float32), dests)
    grid_out = outs.reshape(-1, width)
    grad_grid = grads.reshape(-1, width)
    d_mesh = jnp.dot(d_src.astype(jnp.bfloat16), w_src.T, preferred_element_type=jnp.float32)
    d_mesh_b = d_mesh.astype(jnp.bfloat16)
    d_act = jnp.dot(d_mesh_b, w_out.T, preferred_element_type=jnp.float32)
    d_pre = (d_act * silu_grad(pre_act)).astype(jnp.bfloat16)
    contrib = jnp.einsum('bkji,bid->bkjd', adj_blocks.astype(jnp.float32), d_pre.reshape(nblk, 128, width).astype(jnp.float32))
    d_sent = jax.ops.segment_sum(contrib.reshape(-1, 128, width), adj_index.reshape(-1), nblk).reshape(-1, width).astype(jnp.bfloat16)
    d_norm = jnp.dot(d_pre, w_self.T, preferred_element_type=jnp.float32) + jnp.dot(d_sent, w_send.T, preferred_element_type=jnp.float32)
    d_h = scale * (d_norm - normed * lax.optimization_barrier(jnp.mean(d_norm * normed, axis=-1, keepdims=True)))
    grad_mesh = (d_mesh + d_h).astype(jnp.bfloat16)
    return (grid_out, grad_grid, grad_mesh)
```

```python
import functools

import jax
import jax.numpy as jnp
from jax import lax
from jax.experimental import pallas as pl
from jax.experimental.pallas import tpu as pltpu
from jax.sharding import PartitionSpec as P

REACH = 2
CHUNKS = 4
EDGE_CHUNKS = 2
F32 = jnp.float32
BF16 = jnp.bfloat16


def mm(a, b):
    return jnp.dot(a, b, preferred_element_type=F32)


def mm_nt(a, b):
    return lax.dot_general(a, b, (((1,), (1,)), ((), ())), preferred_element_type=F32)


def silu_grad(value, sig):
    return sig * (1.0 + value * (1.0 - sig))


def kernel(
    n,
    mesh_hbm,
    grid_hbm,
    cot_hbm,
    w_send_hbm,
    w_self_hbm,
    w_out_hbm,
    w_src_hbm,
    w_dst_hbm,
    w_dec_hbm,
    adj_hbm,
    adj_index,
    idx,
    grid_out_hbm,
    grad_grid_hbm,
    grad_mesh_hbm,
    mesh,
    grid,
    cot,
    w_send,
    w_self,
    w_out,
    w_src,
    w_dst,
    w_dec,
    adj,
    nb,
    pre,
    win,
    dense,
    back_dense,
    held,
    pick,
    pick_t,
    join,
    join_t,
    dproj,
    dsum,
    mesh_out,
    rows_out,
    rows_in,
    edge,
    d_edge,
    back,
    sgrad,
    d_mesh,
    d_pre,
    g_own,
    g_two,
    g_three,
    k_out,
    k_in,
    z_out,
    z_in,
    y_out,
    y_in,
    res_a,
    res_b,
    res_c,
    load_sem,
    store_sem,
    idx_send,
    idx_recv,
    win_send,
    win_recv,
    row_send,
    row_recv,
    back_send,
    back_recv,
    k_send,
    k_recv,
    z_send,
    z_recv,
    y_send,
    y_recv,
):
    per_dev, width = mesh.shape
    grid_rows = grid.shape[0]
    blocks, neighbours = adj.shape[0], adj.shape[1]
    cw = width // CHUNKS
    ew = width // EDGE_CHUNKS
    me = lax.axis_index("blk")
    core = lax.rem(me, 2)
    odd = lax.rem(me // 2, 2)
    side = 1 - 2 * odd

    def at(offset):
        return {"blk": lax.rem(me + offset + n, n)}

    mate = at(1 - 2 * core)
    y_mate = at(2 * side)
    ahead = at(4 * side)
    behind = at(-4 * side)
    turn = lax.rem(core + odd, 2)
    passed = 2 + turn
    turn32 = turn.astype(F32)

    barrier = pltpu.get_barrier_semaphore()
    for offset in (-4, -2, -1, 1, 2, 4):
        pl.semaphore_signal(barrier, inc=1, device_id=at(offset), device_id_type=pl.DeviceIdType.MESH)

    pairs = [
        (mesh_hbm, mesh),
        (w_send_hbm, w_send),
        (adj_hbm, adj),
        (w_self_hbm, w_self),
        (grid_hbm, grid),
        (w_dst_hbm, w_dst),
        (cot_hbm, cot),
        (w_dec_hbm, w_dec),
        (w_out_hbm, w_out),
        (w_src_hbm, w_src),
    ]
    loads = [pltpu.make_async_copy(a, b, load_sem.at[i]) for i, (a, b) in enumerate(pairs)]
    for copy in loads:
        copy.start()

    def remote(src, dst, send, recv, device):
        return pltpu.make_async_remote_copy(
            src_ref=src,
            dst_ref=dst,
            send_sem=send,
            recv_sem=recv,
            device_id=device,
            device_id_type=pl.DeviceIdType.MESH,
        )

    loads[0].wait()
    h32 = mesh[...].astype(F32)
    scale = lax.rsqrt(jnp.mean(h32 * h32, axis=-1, keepdims=True) + 1e-05)
    nb[...] = (h32 * scale).astype(BF16)
    loads[1].wait()

    sends = []

    def panel(chunk, slot, dst_slot, number, device):
        copy = remote(
            win.at[chunk, slot],
            win.at[chunk, dst_slot],
            win_send.at[chunk, number],
            win_recv.at[chunk, dst_slot - 1],
            device,
        )
        copy.start()
        sends.append(copy)

    def arrived(chunk, slot):
        remote(
            win.at[chunk, slot], win.at[chunk, slot], win_send.at[chunk, 0], win_recv.at[chunk, slot - 1], mate
        ).wait_recv()

    for c in range(CHUNKS):
        win[c, 0] = mm(nb[...], w_send[:, c * cw : (c + 1) * cw]).astype(BF16)
        if c == 0:
            pl.semaphore_wait(barrier, 6)
        panel(c, 0, 2, 0, y_mate)
        panel(c, 0, 1, 1, mate)

    idx_copies = []
    for place in range(2 * REACH + 1):
        if place != REACH:
            copy = remote(
                idx.at[place], held.at[place], idx_send.at[place], idx_recv.at[place], at(place - REACH)
            )
            copy.start()
            idx_copies.append(copy)

    def hop_y(c):
        arrived(c, 2)
        panel(c, 2, 3, 2, ahead)

    def hop_core(c):
        arrived(c, 3)
        panel(c, passed, 4, 3, mate)

    loads[2].wait()
    for b in range(blocks):
        slots = []
        for k in range(neighbours):
            named = adj_index[me * blocks + b, k]
            away = lax.rem(named // blocks - me + n, n)
            away = jnp.where(away > REACH, away - n, away)
            slot = jnp.where(
                away == 0,
                0,
                jnp.where(
                    away == 1 - 2 * core,
                    1,
                    jnp.where(away == 2 * side, 2, jnp.where(away == -2 * side, 3, 4)),
                ),
            )
            slots.append(slot * blocks + lax.rem(named, blocks))
        for w in range((2 * REACH + 1) * blocks):
            total = jnp.zeros((128, 128), F32)
            for k in range(neighbours):
                total = total + adj[b, k].astype(F32) * (slots[k] == w).astype(F32)
            dense[b * 128 : (b + 1) * 128, w * 128 : (w + 1) * 128] = total.astype(BF16)
            back_dense[w * 128 : (w + 1) * 128, b * 128 : (b + 1) * 128] = total.astype(BF16)

    hop_y(0)
    loads[3].wait()
    pre[...] = mm(nb[...], w_self[...])
    hop_y(1)
    hop_core(0)

    lanes = lax.broadcasted_iota(jnp.int32, (128, 128), 1).astype(F32)
    subs = lax.broadcasted_iota(jnp.int32, (per_dev, 128), 0).astype(F32)
    for t in range(3):
        row = idx[5, t : t + 1, :].astype(F32)
        whole = jnp.broadcast_to(row, (128, 128))
        hot = (whole.T == lanes).astype(F32).astype(BF16)
        join[t * 128 : (t + 1) * 128, 0:128] = hot
        join[t * 128 : (t + 1) * 128, 128:256] = hot
        join_t[:, t * 128 : (t + 1) * 128] = (whole == subs[:128]).astype(F32).astype(BF16)

    loads[4].wait()
    loads[5].wait()
    proj = mm(grid[...], w_dst[...])
    high = proj.astype(BF16)
    low = (proj - high.astype(F32)).astype(BF16)
    dproj[...] = mm(join[...], jnp.concatenate([high, low], axis=0))
    if CHUNKS > 2:
        hop_y(2)
        hop_core(1)
    loads[6].wait()
    loads[7].wait()
    dsum[...] = mm(join[:, 0:128], mm_nt(cot[...], w_dec[...]).astype(BF16)).astype(BF16)

    for copy in idx_copies:
        copy.wait()
    half = lax.broadcasted_iota(jnp.int32, (1, 128), 1) < 64
    index_rows = []
    for place in range(6):
        if place == REACH:
            index_rows.append(idx[place, 0:1, :])
        elif place == 5:
            index_rows.append(jnp.full((1, 128), -1, jnp.int32))
        else:
            index_rows.append(held[place, 0:1, :])
    for t in range(3):
        row = jnp.where(half, index_rows[2 * t], index_rows[2 * t + 1]).astype(F32)
        whole = jnp.broadcast_to(row, (128, 128))
        turned = whole.T
        for u in range(per_dev // 128):
            pick[t * 128 : (t + 1) * 128, u * 128 : (u + 1) * 128] = (
                (turned == lanes + float(u * 128)).astype(F32).astype(BF16)
            )
        pick_t[:, t * 128 : (t + 1) * 128] = (jnp.broadcast_to(row, (per_dev, 128)) == subs).astype(F32).astype(BF16)
    live = 320
    for e in range(EDGE_CHUNKS):
        edge[e, live:384] = jnp.zeros((64, ew), BF16)
        d_edge[e, live:384] = jnp.zeros((64, ew), BF16)
        back[e, live:384] = jnp.zeros((64, ew), BF16)
    loads[8].wait()
    loads[9].wait()

    def mesh_chunk(c, acc):
        arrived(c, 1)
        arrived(c, 4)
        cols = slice(c * cw, (c + 1) * cw)
        value = pre[:, cols] + mm(dense[...], win[c].reshape(5 * per_dev, cw))
        pre[:, cols] = value
        act = (value * jax.nn.sigmoid(value)).astype(BF16)
        return acc + mm(act, w_out[cols, :])

    acc = mesh[...].astype(F32)
    done_y = min(3, CHUNKS) if CHUNKS > 2 else 2
    done_core = done_y - 1
    for c in range(CHUNKS):
        if done_y < CHUNKS:
            hop_y(done_y)
            done_y += 1
        if done_core < CHUNKS:
            hop_core(done_core)
            done_core += 1
        acc = mesh_chunk(c, acc)
    mesh_out[...] = acc.astype(BF16)

    order = (0, 4, 1, 3)
    for e in range(EDGE_CHUNKS):
        cols = slice(e * ew, (e + 1) * ew)
        src = mm(mesh_out[...], w_src[:, cols]).astype(BF16)
        rows_out[e] = mm(pick[...], src).astype(BF16)
        for place in order:
            rows = pl.ds(place * 64, 64)
            copy = remote(
                rows_out.at[e, rows],
                rows_in.at[e, rows],
                row_send.at[e, place],
                row_recv.at[e, place],
                at(REACH - place),
            )
            copy.start()
            sends.append(copy)

    value = pre[...]
    sgrad[...] = silu_grad(value, jax.nn.sigmoid(value))

    for e in range(EDGE_CHUNKS):
        cols = slice(e * ew, (e + 1) * ew)
        for place in (2, 3, 1, 4, 0):
            rows = slice(place * 64, (place + 1) * 64)
            span = pl.ds(place * 64, 64)
            if place == REACH:
                got = rows_out[e, rows]
            else:
                remote(
                    rows_in.at[e, span], rows_in.at[e, span], row_send.at[e, place], row_recv.at[e, place], mate
                ).wait_recv()
                got = rows_in[e, rows]
            joined = got.astype(F32) + dproj[rows, cols]
            sig = jax.nn.sigmoid(joined)
            edge[e, rows] = (joined * sig).astype(BF16)
            grad = (dsum[rows, cols].astype(F32) * silu_grad(joined, sig)).astype(BF16)
            d_edge[e, rows] = grad
            if place == REACH:
                back[e, rows] = grad
            else:
                copy = remote(
                    d_edge.at[e, span],
                    back.at[e, span],
                    back_send.at[e, place],
                    back_recv.at[e, place],
                    at(place - REACH),
                )
                copy.start()
                sends.append(copy)

    out_acc = grid[...].astype(F32)
    grad_acc = cot[...].astype(F32)
    for e in range(EDGE_CHUNKS):
        cols = slice(e * ew, (e + 1) * ew)
        out_acc += mm(mm(join_t[...], edge[e]).astype(BF16), w_dec[cols, :])
        grad_acc += mm_nt(mm(join_t[...], d_edge[e]).astype(BF16), w_dst[:, cols])
    res_a[...] = out_acc.astype(BF16)
    res_b[...] = grad_acc.astype(BF16)
    out_a = pltpu.make_async_copy(res_a, grid_out_hbm, store_sem.at[0])
    out_b = pltpu.make_async_copy(res_b, grad_grid_hbm, store_sem.at[1])
    out_a.start()
    out_b.start()

    acc = jnp.zeros((per_dev, width), F32)
    for e in range(EDGE_CHUNKS):
        cols = slice(e * ew, (e + 1) * ew)
        for place in (3, 1, 4, 0):
            span = pl.ds(place * 64, 64)
            remote(
                back.at[e, span], back.at[e, span], back_send.at[e, place], back_recv.at[e, place], mate
            ).wait_recv()
        acc += mm_nt(mm(pick_t[...], back[e]).astype(BF16), w_src[:, cols])
    d_mesh[...] = acc
    mesh_out[...] = acc.astype(BF16)

    def spread(c):
        cols = slice(c * cw, (c + 1) * cw)
        slope = (mm_nt(mesh_out[...], w_out[cols, :]) * sgrad[:, cols]).astype(BF16)
        d_pre[:, cols] = slope

        def product(slot):
            return mm(back_dense[slot * per_dev : (slot + 1) * per_dev, :], slope)

        k_out[c, 1] = product(4).astype(BF16)
        copy = remote(k_out.at[c, 1], k_in.at[c, 1], k_send.at[c, 1], k_recv.at[c, 1], mate)
        copy.start()
        sends.append(copy)
        k_out[c, 0] = product(1).astype(BF16)
        copy = remote(k_out.at[c, 0], k_in.at[c, 0], k_send.at[c, 0], k_recv.at[c, 0], mate)
        copy.start()
        sends.append(copy)
        g_three[c] = product(3)
        g_two[c] = product(2)
        g_own[c] = product(0)

    def fold_core(c):
        remote(k_out.at[c, 1], k_in.at[c, 1], k_send.at[c, 1], k_recv.at[c, 1], mate).wait_recv()
        came = k_in[c, 1].astype(F32)
        z_out[c] = (g_three[c] + came * turn32).astype(BF16)
        copy = remote(z_out.at[c], z_in.at[c], z_send.at[c], z_recv.at[c], behind)
        copy.start()
        sends.append(copy)
        g_two[c] = g_two[c] + came * (1.0 - turn32)

    def fold_z(c):
        remote(z_out.at[c], z_in.at[c], z_send.at[c], z_recv.at[c], behind).wait_recv()
        y_out[c] = (g_two[c] + z_in[c].astype(F32)).astype(BF16)
        copy = remote(y_out.at[c], y_in.at[c], y_send.at[c], y_recv.at[c], y_mate)
        copy.start()
        sends.append(copy)

    def fold_y(c):
        remote(k_out.at[c, 0], k_in.at[c, 0], k_send.at[c, 0], k_recv.at[c, 0], mate).wait_recv()
        remote(y_out.at[c], y_in.at[c], y_send.at[c], y_recv.at[c], y_mate).wait_recv()
        total = g_own[c] + k_in[c, 0].astype(F32) + y_in[c].astype(F32)
        return mm_nt(total.astype(BF16), w_send[:, c * cw : (c + 1) * cw])

    acc = None
    for step in range(CHUNKS + 3):
        if step < CHUNKS:
            spread(step)
        if 0 <= step - 1 < CHUNKS:
            fold_core(step - 1)
        if 0 <= step - 2 < CHUNKS:
            fold_z(step - 2)
        if step == CHUNKS:
            acc = mm_nt(d_pre[...], w_self[...])
        if step == CHUNKS + 1:
            for c in range(CHUNKS - 2):
                acc += fold_y(c)
    for c in range(max(CHUNKS - 2, 0), CHUNKS):
        acc += fold_y(c)

    h32 = mesh[...].astype(F32)
    scale = lax.rsqrt(jnp.mean(h32 * h32, axis=-1, keepdims=True) + 1e-05)
    normed = h32 * scale
    res_c[...] = (
        d_mesh[...] + scale * (acc - normed * jnp.mean(acc * normed, axis=-1, keepdims=True))
    ).astype(BF16)
    out_c = pltpu.make_async_copy(res_c, grad_mesh_hbm, store_sem.at[2])
    out_c.start()
    for copy in sends:
        copy.wait_send()
    out_a.wait()
    out_b.wait()
    out_c.wait()


def body(
    mesh_in,
    grid_in,
    cotangent,
    w_send,
    w_self,
    w_out,
    w_src,
    w_dst,
    w_dec,
    adj_blocks,
    adj_index,
    src_rows,
    dst_rows,
    counts,
):
    n = lax.axis_size("blk")
    per_dev, width = mesh_in.shape
    grid_rows = grid_in.shape[0]
    places, slots = src_rows.shape[1], src_rows.shape[2]
    cw, ew = width // CHUNKS, width // EDGE_CHUNKS
    src = jnp.concatenate([src_rows[0], src_rows[0]], axis=-1)
    src = jnp.broadcast_to(src[:, None, :], (places, 8, 2 * slots))
    alive = jnp.arange(slots, dtype=jnp.int32)[None, :] < counts[0][:, None]
    dst = jnp.where(alive, dst_rows[0], -1)
    dst = jnp.pad(dst, ((0, 11), (0, 0)), constant_values=-1).reshape(1, 8, 2 * slots)
    idx = jnp.concatenate([src, dst], axis=0)

    def vmem(*shape, dtype=BF16):
        return pltpu.VMEM(shape, dtype)

    dma = pltpu.SemaphoreType.DMA
    weight = vmem(width, width)
    pad = 384
    scratch = [
        vmem(per_dev, width),
        vmem(grid_rows, width),
        vmem(grid_rows, width),
        weight,
        weight,
        weight,
        weight,
        weight,
        weight,
        vmem(*adj_blocks.shape),
        vmem(per_dev, width),
        vmem(per_dev, width, dtype=F32),
        vmem(CHUNKS, 5, per_dev, cw),
        vmem(per_dev, 5 * per_dev),
        vmem(5 * per_dev, per_dev),
        vmem(5, 8, 128, dtype=jnp.int32),
        vmem(pad, per_dev),
        vmem(per_dev, pad),
        vmem(pad, 2 * grid_rows),
        vmem(grid_rows, pad),
        vmem(pad, width, dtype=F32),
        vmem(pad, width),
        vmem(per_dev, width),
        vmem(EDGE_CHUNKS, pad, ew),
        vmem(EDGE_CHUNKS, pad, ew),
        vmem(EDGE_CHUNKS, pad, ew),
        vmem(EDGE_CHUNKS, pad, ew),
        vmem(EDGE_CHUNKS, pad, ew),
        vmem(per_dev, width, dtype=F32),
        vmem(per_dev, width, dtype=F32),
        vmem(per_dev, width),
        vmem(CHUNKS, per_dev, cw, dtype=F32),
        vmem(CHUNKS, per_dev, cw, dtype=F32),
        vmem(CHUNKS, per_dev, cw, dtype=F32),
        vmem(CHUNKS, 2, per_dev, cw),
        vmem(CHUNKS, 2, per_dev, cw),
        vmem(CHUNKS, per_dev, cw),
        vmem(CHUNKS, per_dev, cw),
        vmem(CHUNKS, per_dev, cw),
        vmem(CHUNKS, per_dev, cw),
        vmem(grid_rows, width),
        vmem(grid_rows, width),
        vmem(per_dev, width),
        dma((10,)),
        dma((3,)),
        dma((5,)),
        dma((5,)),
        dma((CHUNKS, 4)),
        dma((CHUNKS, 4)),
        dma((EDGE_CHUNKS, 5)),
        dma((EDGE_CHUNKS, 5)),
        dma((EDGE_CHUNKS, 5)),
        dma((EDGE_CHUNKS, 5)),
        dma((CHUNKS, 2)),
        dma((CHUNKS, 2)),
        dma((CHUNKS,)),
        dma((CHUNKS,)),
        dma((CHUNKS,)),
        dma((CHUNKS,)),
    ]
    hbm = pl.BlockSpec(memory_space=pl.ANY)
    return pl.pallas_call(
        functools.partial(kernel, n),
        out_shape=(
            jax.ShapeDtypeStruct(grid_in.shape, BF16),
            jax.ShapeDtypeStruct(grid_in.shape, BF16),
            jax.ShapeDtypeStruct(mesh_in.shape, BF16),
        ),
        in_specs=[hbm] * 10
        + [pl.BlockSpec(memory_space=pltpu.SMEM), pl.BlockSpec(memory_space=pltpu.VMEM)],
        out_specs=(hbm, hbm, hbm),
        scratch_shapes=scratch,
        compiler_params=pltpu.CompilerParams(
            collective_id=0, has_side_effects=True, vmem_limit_bytes=48 * 1024 * 1024
        ),
    )(
        mesh_in,
        grid_in,
        cotangent,
        w_send,
        w_self,
        w_out,
        w_src,
        w_dst,
        w_dec,
        adj_blocks,
        adj_index,
        idx,
    )


def solution(mesh):
    rows = P(("groups", "blk"), None)
    return jax.shard_map(
        body,
        mesh=mesh,
        in_specs=(rows,) * 3
        + (P(),) * 6
        + (
            P("blk", None, None, None),
            P(),
            P("blk", None, None),
            P("blk", None, None),
            P("blk", None),
        ),
        out_specs=(rows, rows, rows),
        check_vma=False,
    )
```

```python
import functools

import jax
import jax.numpy as jnp
from jax import lax
from jax.experimental import pallas as pl
from jax.experimental.pallas import tpu as pltpu
from jax.sharding import PartitionSpec as P

REACH = 2
CHUNKS = 4
EDGE_CHUNKS = 2
F32 = jnp.float32
BF16 = jnp.bfloat16


def mm(a, b):
    return jnp.dot(a, b, preferred_element_type=F32)


def mm_nt(a, b):
    return lax.dot_general(a, b, (((1,), (1,)), ((), ())), preferred_element_type=F32)


def silu_grad(value, sig):
    return sig * (1.0 + value * (1.0 - sig))


def kernel(
    n,
    mesh_hbm,
    grid_hbm,
    cot_hbm,
    w_send_hbm,
    w_self_hbm,
    w_out_hbm,
    w_src_hbm,
    w_dst_hbm,
    w_dec_hbm,
    adj_hbm,
    adj_index_hbm,
    src_rows,
    dst_rows,
    counts,
    grid_out_hbm,
    grad_grid_hbm,
    grad_mesh_hbm,
    mesh,
    grid,
    cot,
    w_send,
    w_self,
    w_out,
    w_src,
    w_dst,
    w_dec,
    adj,
    adj_index,
    idx,
    nb,
    pre,
    win,
    dense,
    back_dense,
    held,
    pick,
    pick_t,
    join,
    join_t,
    dproj,
    dsum,
    mesh_out,
    rows_out,
    rows_in,
    edge,
    d_edge,
    back,
    sgrad,
    d_mesh,
    d_pre,
    g_own,
    g_two,
    g_three,
    k_out,
    k_in,
    z_out,
    z_in,
    y_out,
    y_in,
    res_a,
    res_b,
    res_c,
    load_sem,
    store_sem,
    idx_send,
    idx_recv,
    win_send,
    win_recv,
    row_send,
    row_recv,
    back_send,
    back_recv,
    k_send,
    k_recv,
    z_send,
    z_recv,
    y_send,
    y_recv,
):
    per_dev, width = mesh.shape
    grid_rows = grid.shape[0]
    blocks, neighbours = adj.shape[0], adj.shape[1]
    cw = width // CHUNKS
    ew = width // EDGE_CHUNKS
    me = lax.axis_index("blk")
    core = lax.rem(me, 2)
    odd = lax.rem(me // 2, 2)
    side = 1 - 2 * odd

    def at(offset):
        return {"blk": lax.rem(me + offset + n, n)}

    mate = at(1 - 2 * core)
    y_mate = at(2 * side)
    ahead = at(4 * side)
    behind = at(-4 * side)
    turn = lax.rem(core + odd, 2)
    passed = 2 + turn
    turn32 = turn.astype(F32)

    barrier = pltpu.get_barrier_semaphore()
    for offset in (-4, -2, -1, 1, 2, 4):
        pl.semaphore_signal(barrier, inc=1, device_id=at(offset), device_id_type=pl.DeviceIdType.MESH)

    pairs = [
        (mesh_hbm, mesh),
        (w_send_hbm, w_send),
        (adj_hbm, adj),
        (w_self_hbm, w_self),
        (grid_hbm, grid),
        (w_dst_hbm, w_dst),
        (cot_hbm, cot),
        (w_dec_hbm, w_dec),
        (w_out_hbm, w_out),
        (w_src_hbm, w_src),
        (adj_index_hbm, adj_index),
    ]
    loads = [pltpu.make_async_copy(a, b, load_sem.at[i]) for i, (a, b) in enumerate(pairs)]
    for copy in loads:
        copy.start()

    def remote(src, dst, send, recv, device):
        return pltpu.make_async_remote_copy(
            src_ref=src,
            dst_ref=dst,
            send_sem=send,
            recv_sem=recv,
            device_id=device,
            device_id_type=pl.DeviceIdType.MESH,
        )

    loads[0].wait()
    h32 = mesh[...].astype(F32)
    scale = lax.rsqrt(jnp.mean(h32 * h32, axis=-1, keepdims=True) + 1e-05)
    nb[...] = (h32 * scale).astype(BF16)
    loads[1].wait()

    sends = []

    def panel(chunk, slot, dst_slot, number, device):
        copy = remote(
            win.at[chunk, slot],
            win.at[chunk, dst_slot],
            win_send.at[chunk, number],
            win_recv.at[chunk, dst_slot - 1],
            device,
        )
        copy.start()
        sends.append(copy)

    def arrived(chunk, slot):
        remote(
            win.at[chunk, slot], win.at[chunk, slot], win_send.at[chunk, 0], win_recv.at[chunk, slot - 1], mate
        ).wait_recv()

    for c in range(CHUNKS):
        win[c, 0] = mm(nb[...], w_send[:, c * cw : (c + 1) * cw]).astype(BF16)
        if c == 0:
            pl.semaphore_wait(barrier, 6)
        panel(c, 0, 2, 0, y_mate)
        panel(c, 0, 1, 1, mate)

    spot = lax.broadcasted_iota(jnp.int32, (1, 64), 1)
    idx[5] = jnp.full((8, 128), -1, jnp.int32)
    for place in range(2 * REACH + 1):
        row = jnp.broadcast_to(src_rows[0, place : place + 1, :], (8, 64))
        idx[place, :, 0:64] = row
        idx[place, :, 64:128] = row
        alive = spot < counts[0:1, place : place + 1]
        column = place % 2 * 64
        idx[5, place // 2 : place // 2 + 1, column : column + 64] = jnp.where(
            alive, dst_rows[0, place : place + 1, :], -1
        )
    idx_copies = []
    for place in range(2 * REACH + 1):
        if place != REACH:
            copy = remote(
                idx.at[place], held.at[place], idx_send.at[place], idx_recv.at[place], at(place - REACH)
            )
            copy.start()
            idx_copies.append(copy)

    def hop_y(c):
        arrived(c, 2)
        panel(c, 2, 3, 2, ahead)

    def hop_core(c):
        arrived(c, 3)
        panel(c, passed, 4, 3, mate)

    loads[2].wait()
    loads[10].wait()
    for b in range(blocks):
        slots = []
        for k in range(neighbours):
            named = adj_index[me * blocks + b, k]
            away = lax.rem(named // blocks - me + n, n)
            away = jnp.where(away > REACH, away - n, away)
            slot = jnp.where(
                away == 0,
                0,
                jnp.where(
                    away == 1 - 2 * core,
                    1,
                    jnp.where(away == 2 * side, 2, jnp.where(away == -2 * side, 3, 4)),
                ),
            )
            slots.append(slot * blocks + lax.rem(named, blocks))
        for w in range((2 * REACH + 1) * blocks):
            total = jnp.zeros((128, 128), F32)
            for k in range(neighbours):
                total = total + adj[b, k].astype(F32) * (slots[k] == w).astype(F32)
            dense[b * 128 : (b + 1) * 128, w * 128 : (w + 1) * 128] = total.astype(BF16)
            back_dense[w * 128 : (w + 1) * 128, b * 128 : (b + 1) * 128] = total.astype(BF16)

    hop_y(0)
    loads[3].wait()
    pre[...] = mm(nb[...], w_self[...])
    hop_y(1)
    hop_core(0)

    lanes = lax.broadcasted_iota(jnp.int32, (128, 128), 1).astype(F32)
    subs = lax.broadcasted_iota(jnp.int32, (per_dev, 128), 0).astype(F32)
    for t in range(3):
        row = idx[5, t : t + 1, :].astype(F32)
        whole = jnp.broadcast_to(row, (128, 128))
        hot = (whole.T == lanes).astype(F32).astype(BF16)
        join[t * 128 : (t + 1) * 128, 0:128] = hot
        join[t * 128 : (t + 1) * 128, 128:256] = hot
        join_t[:, t * 128 : (t + 1) * 128] = (whole == subs[:128]).astype(F32).astype(BF16)

    loads[4].wait()
    loads[5].wait()
    proj = mm(grid[...], w_dst[...])
    high = proj.astype(BF16)
    low = (proj - high.astype(F32)).astype(BF16)
    dproj[...] = mm(join[...], jnp.concatenate([high, low], axis=0))
    if CHUNKS > 2:
        hop_y(2)
        hop_core(1)
    loads[6].wait()
    loads[7].wait()
    dsum[...] = mm(join[:, 0:128], mm_nt(cot[...], w_dec[...]).astype(BF16)).astype(BF16)

    for copy in idx_copies:
        copy.wait()
    half = lax.broadcasted_iota(jnp.int32, (1, 128), 1) < 64
    index_rows = []
    for place in range(6):
        if place == REACH:
            index_rows.append(idx[place, 0:1, :])
        elif place == 5:
            index_rows.append(jnp.full((1, 128), -1, jnp.int32))
        else:
            index_rows.append(held[place, 0:1, :])
    for t in range(3):
        row = jnp.where(half, index_rows[2 * t], index_rows[2 * t + 1]).astype(F32)
        whole = jnp.broadcast_to(row, (128, 128))
        turned = whole.T
        for u in range(per_dev // 128):
            pick[t * 128 : (t + 1) * 128, u * 128 : (u + 1) * 128] = (
                (turned == lanes + float(u * 128)).astype(F32).astype(BF16)
            )
        pick_t[:, t * 128 : (t + 1) * 128] = (jnp.broadcast_to(row, (per_dev, 128)) == subs).astype(F32).astype(BF16)
    live = 320
    for e in range(EDGE_CHUNKS):
        edge[e, live:384] = jnp.zeros((64, ew), BF16)
        d_edge[e, live:384] = jnp.zeros((64, ew), BF16)
        back[e, live:384] = jnp.zeros((64, ew), BF16)
    loads[8].wait()
    loads[9].wait()

    def mesh_chunk(c, acc):
        arrived(c, 1)
        arrived(c, 4)
        cols = slice(c * cw, (c + 1) * cw)
        value = pre[:, cols] + mm(dense[...], win[c].reshape(5 * per_dev, cw))
        pre[:, cols] = value
        act = (value * jax.nn.sigmoid(value)).astype(BF16)
        return acc + mm(act, w_out[cols, :])

    acc = mesh[...].astype(F32)
    done_y = min(3, CHUNKS) if CHUNKS > 2 else 2
    done_core = done_y - 1
    for c in range(CHUNKS):
        if done_y < CHUNKS:
            hop_y(done_y)
            done_y += 1
        if done_core < CHUNKS:
            hop_core(done_core)
            done_core += 1
        acc = mesh_chunk(c, acc)
    mesh_out[...] = acc.astype(BF16)

    order = (0, 4, 1, 3)
    for e in range(EDGE_CHUNKS):
        cols = slice(e * ew, (e + 1) * ew)
        src = mm(mesh_out[...], w_src[:, cols]).astype(BF16)
        rows_out[e] = mm(pick[...], src).astype(BF16)
        for place in order:
            rows = pl.ds(place * 64, 64)
            copy = remote(
                rows_out.at[e, rows],
                rows_in.at[e, rows],
                row_send.at[e, place],
                row_recv.at[e, place],
                at(REACH - place),
            )
            copy.start()
            sends.append(copy)

    value = pre[...]
    sgrad[...] = silu_grad(value, jax.nn.sigmoid(value))

    for e in range(EDGE_CHUNKS):
        cols = slice(e * ew, (e + 1) * ew)
        for place in (2, 3, 1, 4, 0):
            rows = slice(place * 64, (place + 1) * 64)
            span = pl.ds(place * 64, 64)
            if place == REACH:
                got = rows_out[e, rows]
            else:
                remote(
                    rows_in.at[e, span], rows_in.at[e, span], row_send.at[e, place], row_recv.at[e, place], mate
                ).wait_recv()
                got = rows_in[e, rows]
            joined = got.astype(F32) + dproj[rows, cols]
            sig = jax.nn.sigmoid(joined)
            edge[e, rows] = (joined * sig).astype(BF16)
            grad = (dsum[rows, cols].astype(F32) * silu_grad(joined, sig)).astype(BF16)
            d_edge[e, rows] = grad
            if place == REACH:
                back[e, rows] = grad
            else:
                copy = remote(
                    d_edge.at[e, span],
                    back.at[e, span],
                    back_send.at[e, place],
                    back_recv.at[e, place],
                    at(place - REACH),
                )
                copy.start()
                sends.append(copy)

    out_acc = grid[...].astype(F32)
    grad_acc = cot[...].astype(F32)
    for e in range(EDGE_CHUNKS):
        cols = slice(e * ew, (e + 1) * ew)
        out_acc += mm(mm(join_t[...], edge[e]).astype(BF16), w_dec[cols, :])
        grad_acc += mm_nt(mm(join_t[...], d_edge[e]).astype(BF16), w_dst[:, cols])
    res_a[...] = out_acc.astype(BF16)
    res_b[...] = grad_acc.astype(BF16)
    out_a = pltpu.make_async_copy(res_a, grid_out_hbm, store_sem.at[0])
    out_b = pltpu.make_async_copy(res_b, grad_grid_hbm, store_sem.at[1])
    out_a.start()
    out_b.start()

    acc = jnp.zeros((per_dev, width), F32)
    for e in range(EDGE_CHUNKS):
        cols = slice(e * ew, (e + 1) * ew)
        for place in (3, 1, 4, 0):
            span = pl.ds(place * 64, 64)
            remote(
                back.at[e, span], back.at[e, span], back_send.at[e, place], back_recv.at[e, place], mate
            ).wait_recv()
        acc += mm_nt(mm(pick_t[...], back[e]).astype(BF16), w_src[:, cols])
    d_mesh[...] = acc
    mesh_out[...] = acc.astype(BF16)

    def spread(c):
        cols = slice(c * cw, (c + 1) * cw)
        slope = (mm_nt(mesh_out[...], w_out[cols, :]) * sgrad[:, cols]).astype(BF16)
        d_pre[:, cols] = slope

        def product(slot):
            return mm(back_dense[slot * per_dev : (slot + 1) * per_dev, :], slope)

        k_out[c, 1] = product(4).astype(BF16)
        copy = remote(k_out.at[c, 1], k_in.at[c, 1], k_send.at[c, 1], k_recv.at[c, 1], mate)
        copy.start()
        sends.append(copy)
        k_out[c, 0] = product(1).astype(BF16)
        copy = remote(k_out.at[c, 0], k_in.at[c, 0], k_send.at[c, 0], k_recv.at[c, 0], mate)
        copy.start()
        sends.append(copy)
        g_three[c] = product(3)
        g_two[c] = product(2)
        g_own[c] = product(0)

    def fold_core(c):
        remote(k_out.at[c, 1], k_in.at[c, 1], k_send.at[c, 1], k_recv.at[c, 1], mate).wait_recv()
        came = k_in[c, 1].astype(F32)
        z_out[c] = (g_three[c] + came * turn32).astype(BF16)
        copy = remote(z_out.at[c], z_in.at[c], z_send.at[c], z_recv.at[c], behind)
        copy.start()
        sends.append(copy)
        g_two[c] = g_two[c] + came * (1.0 - turn32)

    def fold_z(c):
        remote(z_out.at[c], z_in.at[c], z_send.at[c], z_recv.at[c], behind).wait_recv()
        y_out[c] = (g_two[c] + z_in[c].astype(F32)).astype(BF16)
        copy = remote(y_out.at[c], y_in.at[c], y_send.at[c], y_recv.at[c], y_mate)
        copy.start()
        sends.append(copy)

    def fold_y(c):
        remote(k_out.at[c, 0], k_in.at[c, 0], k_send.at[c, 0], k_recv.at[c, 0], mate).wait_recv()
        remote(y_out.at[c], y_in.at[c], y_send.at[c], y_recv.at[c], y_mate).wait_recv()
        total = g_own[c] + k_in[c, 0].astype(F32) + y_in[c].astype(F32)
        return mm_nt(total.astype(BF16), w_send[:, c * cw : (c + 1) * cw])

    acc = None
    for step in range(CHUNKS + 3):
        if step < CHUNKS:
            spread(step)
        if 0 <= step - 1 < CHUNKS:
            fold_core(step - 1)
        if 0 <= step - 2 < CHUNKS:
            fold_z(step - 2)
        if step == CHUNKS:
            acc = mm_nt(d_pre[...], w_self[...])
        if step == CHUNKS + 1:
            for c in range(CHUNKS - 2):
                acc += fold_y(c)
    for c in range(max(CHUNKS - 2, 0), CHUNKS):
        acc += fold_y(c)

    h32 = mesh[...].astype(F32)
    scale = lax.rsqrt(jnp.mean(h32 * h32, axis=-1, keepdims=True) + 1e-05)
    normed = h32 * scale
    res_c[...] = (
        d_mesh[...] + scale * (acc - normed * jnp.mean(acc * normed, axis=-1, keepdims=True))
    ).astype(BF16)
    out_c = pltpu.make_async_copy(res_c, grad_mesh_hbm, store_sem.at[2])
    out_c.start()
    for copy in sends:
        copy.wait_send()
    out_a.wait()
    out_b.wait()
    out_c.wait()


def body(
    mesh_in,
    grid_in,
    cotangent,
    w_send,
    w_self,
    w_out,
    w_src,
    w_dst,
    w_dec,
    adj_blocks,
    adj_index,
    src_rows,
    dst_rows,
    counts,
):
    n = lax.axis_size("blk")
    per_dev, width = mesh_in.shape
    grid_rows = grid_in.shape[0]
    cw, ew = width // CHUNKS, width // EDGE_CHUNKS
    def vmem(*shape, dtype=BF16):
        return pltpu.VMEM(shape, dtype)

    dma = pltpu.SemaphoreType.DMA
    weight = vmem(width, width)
    pad = 384
    scratch = [
        vmem(per_dev, width),
        vmem(grid_rows, width),
        vmem(grid_rows, width),
        weight,
        weight,
        weight,
        weight,
        weight,
        weight,
        vmem(*adj_blocks.shape),
        pltpu.SMEM(adj_index.shape, jnp.int32),
        vmem(6, 8, 128, dtype=jnp.int32),
        vmem(per_dev, width),
        vmem(per_dev, width, dtype=F32),
        vmem(CHUNKS, 5, per_dev, cw),
        vmem(per_dev, 5 * per_dev),
        vmem(5 * per_dev, per_dev),
        vmem(5, 8, 128, dtype=jnp.int32),
        vmem(pad, per_dev),
        vmem(per_dev, pad),
        vmem(pad, 2 * grid_rows),
        vmem(grid_rows, pad),
        vmem(pad, width, dtype=F32),
        vmem(pad, width),
        vmem(per_dev, width),
        vmem(EDGE_CHUNKS, pad, ew),
        vmem(EDGE_CHUNKS, pad, ew),
        vmem(EDGE_CHUNKS, pad, ew),
        vmem(EDGE_CHUNKS, pad, ew),
        vmem(EDGE_CHUNKS, pad, ew),
        vmem(per_dev, width, dtype=F32),
        vmem(per_dev, width, dtype=F32),
        vmem(per_dev, width),
        vmem(CHUNKS, per_dev, cw, dtype=F32),
        vmem(CHUNKS, per_dev, cw, dtype=F32),
        vmem(CHUNKS, per_dev, cw, dtype=F32),
        vmem(CHUNKS, 2, per_dev, cw),
        vmem(CHUNKS, 2, per_dev, cw),
        vmem(CHUNKS, per_dev, cw),
        vmem(CHUNKS, per_dev, cw),
        vmem(CHUNKS, per_dev, cw),
        vmem(CHUNKS, per_dev, cw),
        vmem(grid_rows, width),
        vmem(grid_rows, width),
        vmem(per_dev, width),
        dma((11,)),
        dma((3,)),
        dma((5,)),
        dma((5,)),
        dma((CHUNKS, 4)),
        dma((CHUNKS, 4)),
        dma((EDGE_CHUNKS, 5)),
        dma((EDGE_CHUNKS, 5)),
        dma((EDGE_CHUNKS, 5)),
        dma((EDGE_CHUNKS, 5)),
        dma((CHUNKS, 2)),
        dma((CHUNKS, 2)),
        dma((CHUNKS,)),
        dma((CHUNKS,)),
        dma((CHUNKS,)),
        dma((CHUNKS,)),
    ]
    hbm = pl.BlockSpec(memory_space=pltpu.HBM)
    return pl.pallas_call(
        functools.partial(kernel, n),
        out_shape=(
            jax.ShapeDtypeStruct(grid_in.shape, BF16),
            jax.ShapeDtypeStruct(grid_in.shape, BF16),
            jax.ShapeDtypeStruct(mesh_in.shape, BF16),
        ),
        in_specs=[hbm] * 11 + [pl.BlockSpec(memory_space=pltpu.VMEM)] * 3,
        out_specs=(hbm, hbm, hbm),
        scratch_shapes=scratch,
        compiler_params=pltpu.CompilerParams(
            collective_id=0, has_side_effects=True, vmem_limit_bytes=64 * 1024 * 1024 - 65536
        ),
    )(
        mesh_in,
        grid_in,
        cotangent,
        w_send,
        w_self,
        w_out,
        w_src,
        w_dst,
        w_dec,
        adj_blocks,
        adj_index,
        src_rows,
        dst_rows,
        counts,
    )


def solution(mesh):
    rows = P(("groups", "blk"), None)
    return jax.shard_map(
        body,
        mesh=mesh,
        in_specs=(rows,) * 3
        + (P(),) * 6
        + (
            P("blk", None, None, None),
            P(),
            P("blk", None, None),
            P("blk", None, None),
            P("blk", None),
        ),
        out_specs=(rows, rows, rows),
        check_vma=False,
    )
```

```python
import functools

import jax
import jax.numpy as jnp
from jax import lax
from jax.experimental import pallas as pl
from jax.experimental.pallas import tpu as pltpu
from jax.sharding import PartitionSpec as P

REACH = 2
CHUNKS = 4
EDGE_CHUNKS = 2
F32 = jnp.float32
BF16 = jnp.bfloat16


def mm(a, b):
    return jnp.dot(a, b, preferred_element_type=F32)


def mm_nt(a, b):
    return lax.dot_general(a, b, (((1,), (1,)), ((), ())), preferred_element_type=F32)


def silu_grad(value, sig):
    return sig * (1.0 + value * (1.0 - sig))


def kernel(
    n,
    mesh_hbm,
    grid_hbm,
    cot_hbm,
    w_send_hbm,
    w_self_hbm,
    w_out_hbm,
    w_src_hbm,
    w_dst_hbm,
    w_dec_hbm,
    adj_hbm,
    adj_index_hbm,
    src_rows,
    dst_rows,
    counts,
    grid_out_hbm,
    grad_grid_hbm,
    grad_mesh_hbm,
    mesh,
    grid,
    cot,
    w_send,
    w_self,
    w_out,
    w_src,
    w_dst,
    w_dec,
    adj,
    adj_index,
    idx,
    nb,
    pre,
    win,
    dense,
    back_dense,
    held,
    pick,
    pick_t,
    join,
    join_t,
    dproj,
    dsum,
    mesh_out,
    rows_out,
    rows_in,
    edge,
    d_edge,
    back,
    sgrad,
    d_mesh,
    d_pre,
    g_own,
    g_two,
    g_three,
    k_out,
    k_in,
    z_out,
    z_in,
    y_out,
    y_in,
    res_a,
    res_b,
    res_c,
    load_sem,
    store_sem,
    idx_send,
    idx_recv,
    win_send,
    win_recv,
    row_send,
    row_recv,
    back_send,
    back_recv,
    k_send,
    k_recv,
    z_send,
    z_recv,
    y_send,
    y_recv,
):
    per_dev, width = mesh.shape
    grid_rows = grid.shape[0]
    blocks, neighbours = adj.shape[0], adj.shape[1]
    cw = width // CHUNKS
    ew = width // EDGE_CHUNKS
    me = lax.axis_index("blk")
    core = lax.rem(me, 2)
    odd = lax.rem(me // 2, 2)
    side = 1 - 2 * odd

    def at(offset):
        return {"blk": lax.rem(me + offset + n, n)}

    mate = at(1 - 2 * core)
    y_mate = at(2 * side)
    ahead = at(4 * side)
    behind = at(-4 * side)
    turn = lax.rem(core + odd, 2)
    passed = 2 + turn
    turn32 = turn.astype(F32)

    barrier = pltpu.get_barrier_semaphore()
    for offset in (-4, -2, -1, 1, 2, 4):
        pl.semaphore_signal(barrier, inc=1, device_id=at(offset), device_id_type=pl.DeviceIdType.MESH)

    pairs = [
        (mesh_hbm, mesh),
        (w_send_hbm, w_send),
        (adj_hbm, adj),
        (w_self_hbm, w_self),
        (grid_hbm, grid),
        (w_dst_hbm, w_dst),
        (cot_hbm, cot),
        (w_dec_hbm, w_dec),
        (w_out_hbm, w_out),
        (w_src_hbm, w_src),
        (adj_index_hbm, adj_index),
    ]
    loads = [pltpu.make_async_copy(a, b, load_sem.at[i]) for i, (a, b) in enumerate(pairs)]
    for copy in loads:
        copy.start()

    def remote(src, dst, send, recv, device):
        return pltpu.make_async_remote_copy(
            src_ref=src,
            dst_ref=dst,
            send_sem=send,
            recv_sem=recv,
            device_id=device,
            device_id_type=pl.DeviceIdType.MESH,
        )

    loads[0].wait()
    h32 = mesh[...].astype(F32)
    scale = lax.rsqrt(jnp.mean(h32 * h32, axis=-1, keepdims=True) + 1e-05)
    nb[...] = (h32 * scale).astype(BF16)
    loads[1].wait()

    sends = []

    def panel(chunk, slot, dst_slot, number, device):
        copy = remote(
            win.at[chunk, slot],
            win.at[chunk, dst_slot],
            win_send.at[chunk, number],
            win_recv.at[chunk, dst_slot - 1],
            device,
        )
        copy.start()
        sends.append(copy)

    def arrived(chunk, slot):
        remote(
            win.at[chunk, slot], win.at[chunk, slot], win_send.at[chunk, 0], win_recv.at[chunk, slot - 1], mate
        ).wait_recv()

    for c in range(CHUNKS):
        win[c, 0] = mm(nb[...], w_send[:, c * cw : (c + 1) * cw]).astype(BF16)
        if c == 0:
            pl.semaphore_wait(barrier, 6)
        panel(c, 0, 2, 0, y_mate)
        panel(c, 0, 1, 1, mate)

    spot = lax.broadcasted_iota(jnp.int32, (1, 64), 1)
    idx[5] = jnp.full((8, 128), -1, jnp.int32)
    for place in range(2 * REACH + 1):
        row = jnp.broadcast_to(src_rows[0, place : place + 1, :], (8, 64))
        idx[place, :, 0:64] = row
        idx[place, :, 64:128] = row
        alive = spot < counts[0:1, place : place + 1]
        column = place % 2 * 64
        idx[5, place // 2 : place // 2 + 1, column : column + 64] = jnp.where(
            alive, dst_rows[0, place : place + 1, :], -1
        )
    idx_copies = []
    for place in range(2 * REACH + 1):
        if place != REACH:
            copy = remote(
                idx.at[place], held.at[place], idx_send.at[place], idx_recv.at[place], at(place - REACH)
            )
            copy.start()
            idx_copies.append(copy)

    def hop_y(c):
        arrived(c, 2)
        panel(c, 2, 3, 2, ahead)

    def hop_core(c):
        arrived(c, 3)
        panel(c, passed, 4, 3, mate)

    loads[2].wait()
    loads[10].wait()
    for b in range(blocks):
        slots = []
        for k in range(neighbours):
            named = adj_index[me * blocks + b, k]
            away = lax.rem(named // blocks - me + n, n)
            away = jnp.where(away > REACH, away - n, away)
            slot = jnp.where(
                away == 0,
                0,
                jnp.where(
                    away == 1 - 2 * core,
                    1,
                    jnp.where(away == 2 * side, 2, jnp.where(away == -2 * side, 3, 4)),
                ),
            )
            slots.append(slot * blocks + lax.rem(named, blocks))
        for w in range((2 * REACH + 1) * blocks):
            total = jnp.zeros((128, 128), F32)
            for k in range(neighbours):
                total = total + adj[b, k].astype(F32) * (slots[k] == w).astype(F32)
            dense[b * 128 : (b + 1) * 128, w * 128 : (w + 1) * 128] = total.astype(BF16)
            back_dense[w * 128 : (w + 1) * 128, b * 128 : (b + 1) * 128] = total.astype(BF16)

    hop_y(0)
    loads[3].wait()
    pre[...] = mm(nb[...], w_self[...])
    hop_y(1)
    hop_core(0)

    lanes = lax.broadcasted_iota(jnp.int32, (128, 128), 1).astype(F32)
    subs = lax.broadcasted_iota(jnp.int32, (per_dev, 128), 0).astype(F32)
    for t in range(3):
        row = idx[5, t : t + 1, :].astype(F32)
        whole = jnp.broadcast_to(row, (128, 128))
        hot = (whole.T == lanes).astype(F32).astype(BF16)
        join[t * 128 : (t + 1) * 128, 0:128] = hot
        join[t * 128 : (t + 1) * 128, 128:256] = hot
        join_t[:, t * 128 : (t + 1) * 128] = (whole == subs[:128]).astype(F32).astype(BF16)

    loads[4].wait()
    loads[5].wait()
    proj = mm(grid[...], w_dst[...])
    high = proj.astype(BF16)
    low = (proj - high.astype(F32)).astype(BF16)
    dproj[...] = mm(join[...], jnp.concatenate([high, low], axis=0))
    hop_y(2)
    hop_core(1)
    loads[6].wait()
    loads[7].wait()
    dsum[...] = mm(join[:, 0:128], mm_nt(cot[...], w_dec[...]).astype(BF16)).astype(BF16)

    hop_y(3)
    hop_core(2)

    for copy in idx_copies:
        copy.wait()
    half = lax.broadcasted_iota(jnp.int32, (1, 128), 1) < 64
    index_rows = []
    for place in range(6):
        if place == REACH:
            index_rows.append(idx[place, 0:1, :])
        elif place == 5:
            index_rows.append(jnp.full((1, 128), -1, jnp.int32))
        else:
            index_rows.append(held[place, 0:1, :])
    for t in range(3):
        row = jnp.where(half, index_rows[2 * t], index_rows[2 * t + 1]).astype(F32)
        whole = jnp.broadcast_to(row, (128, 128))
        turned = whole.T
        for u in range(per_dev // 128):
            pick[t * 128 : (t + 1) * 128, u * 128 : (u + 1) * 128] = (
                (turned == lanes + float(u * 128)).astype(F32).astype(BF16)
            )
        pick_t[:, t * 128 : (t + 1) * 128] = (jnp.broadcast_to(row, (per_dev, 128)) == subs).astype(F32).astype(BF16)
    live = 320
    for e in range(EDGE_CHUNKS):
        edge[e, live:384] = jnp.zeros((64, ew), BF16)
        d_edge[e, live:384] = jnp.zeros((64, ew), BF16)
        back[e, live:384] = jnp.zeros((64, ew), BF16)
    loads[8].wait()
    loads[9].wait()

    def mesh_chunk(c, acc):
        arrived(c, 1)
        arrived(c, 4)
        cols = slice(c * cw, (c + 1) * cw)
        value = pre[:, cols] + mm(dense[...], win[c].reshape(5 * per_dev, cw))
        pre[:, cols] = value
        act = (value * jax.nn.sigmoid(value)).astype(BF16)
        return acc + mm(act, w_out[cols, :])

    acc = mesh[...].astype(F32)
    hop_core(3)
    for c in range(CHUNKS):
        acc = mesh_chunk(c, acc)
    mesh_out[...] = acc.astype(BF16)

    order = (0, 4, 1, 3)
    for e in range(EDGE_CHUNKS):
        cols = slice(e * ew, (e + 1) * ew)
        src = mm(mesh_out[...], w_src[:, cols]).astype(BF16)
        rows_out[e] = mm(pick[...], src).astype(BF16)
        for place in order:
            rows = pl.ds(place * 64, 64)
            copy = remote(
                rows_out.at[e, rows],
                rows_in.at[e, rows],
                row_send.at[e, place],
                row_recv.at[e, place],
                at(REACH - place),
            )
            copy.start()
            sends.append(copy)

    value = pre[...]
    sgrad[...] = silu_grad(value, jax.nn.sigmoid(value))

    for e in range(EDGE_CHUNKS):
        cols = slice(e * ew, (e + 1) * ew)
        for place in (2, 3, 1, 4, 0):
            rows = slice(place * 64, (place + 1) * 64)
            span = pl.ds(place * 64, 64)
            if place == REACH:
                got = rows_out[e, rows]
            else:
                remote(
                    rows_in.at[e, span], rows_in.at[e, span], row_send.at[e, place], row_recv.at[e, place], mate
                ).wait_recv()
                got = rows_in[e, rows]
            joined = got.astype(F32) + dproj[rows, cols]
            sig = jax.nn.sigmoid(joined)
            edge[e, rows] = (joined * sig).astype(BF16)
            grad = (dsum[rows, cols].astype(F32) * silu_grad(joined, sig)).astype(BF16)
            d_edge[e, rows] = grad
            if place == REACH:
                back[e, rows] = grad
            else:
                copy = remote(
                    d_edge.at[e, span],
                    back.at[e, span],
                    back_send.at[e, place],
                    back_recv.at[e, place],
                    at(place - REACH),
                )
                copy.start()
                sends.append(copy)

    out_acc = grid[...].astype(F32)
    grad_acc = cot[...].astype(F32)
    for e in range(EDGE_CHUNKS):
        cols = slice(e * ew, (e + 1) * ew)
        out_acc += mm(mm(join_t[...], edge[e]).astype(BF16), w_dec[cols, :])
        grad_acc += mm_nt(mm(join_t[...], d_edge[e]).astype(BF16), w_dst[:, cols])
    res_a[...] = out_acc.astype(BF16)
    res_b[...] = grad_acc.astype(BF16)
    out_a = pltpu.make_async_copy(res_a, grid_out_hbm, store_sem.at[0])
    out_b = pltpu.make_async_copy(res_b, grad_grid_hbm, store_sem.at[1])
    out_a.start()
    out_b.start()

    acc = jnp.zeros((per_dev, width), F32)
    for e in range(EDGE_CHUNKS):
        cols = slice(e * ew, (e + 1) * ew)
        for place in (3, 1, 4, 0):
            span = pl.ds(place * 64, 64)
            remote(
                back.at[e, span], back.at[e, span], back_send.at[e, place], back_recv.at[e, place], mate
            ).wait_recv()
        acc += mm_nt(mm(pick_t[...], back[e]).astype(BF16), w_src[:, cols])
    d_mesh[...] = acc
    mesh_out[...] = acc.astype(BF16)

    def spread(c):
        cols = slice(c * cw, (c + 1) * cw)
        slope = (mm_nt(mesh_out[...], w_out[cols, :]) * sgrad[:, cols]).astype(BF16)
        d_pre[:, cols] = slope

        def product(slot):
            return mm(back_dense[slot * per_dev : (slot + 1) * per_dev, :], slope)

        k_out[c, 1] = product(4).astype(BF16)
        copy = remote(k_out.at[c, 1], k_in.at[c, 1], k_send.at[c, 1], k_recv.at[c, 1], mate)
        copy.start()
        sends.append(copy)
        k_out[c, 0] = product(1).astype(BF16)
        copy = remote(k_out.at[c, 0], k_in.at[c, 0], k_send.at[c, 0], k_recv.at[c, 0], mate)
        copy.start()
        sends.append(copy)
        g_three[c] = product(3)
        g_two[c] = product(2)
        g_own[c] = product(0)

    def fold_core(c):
        remote(k_out.at[c, 1], k_in.at[c, 1], k_send.at[c, 1], k_recv.at[c, 1], mate).wait_recv()
        came = k_in[c, 1].astype(F32)
        z_out[c] = (g_three[c] + came * turn32).astype(BF16)
        copy = remote(z_out.at[c], z_in.at[c], z_send.at[c], z_recv.at[c], behind)
        copy.start()
        sends.append(copy)
        g_two[c] = g_two[c] + came * (1.0 - turn32)

    def fold_z(c):
        remote(z_out.at[c], z_in.at[c], z_send.at[c], z_recv.at[c], behind).wait_recv()
        y_out[c] = (g_two[c] + z_in[c].astype(F32)).astype(BF16)
        copy = remote(y_out.at[c], y_in.at[c], y_send.at[c], y_recv.at[c], y_mate)
        copy.start()
        sends.append(copy)

    def fold_y(c):
        remote(k_out.at[c, 0], k_in.at[c, 0], k_send.at[c, 0], k_recv.at[c, 0], mate).wait_recv()
        remote(y_out.at[c], y_in.at[c], y_send.at[c], y_recv.at[c], y_mate).wait_recv()
        total = g_own[c] + k_in[c, 0].astype(F32) + y_in[c].astype(F32)
        return mm_nt(total.astype(BF16), w_send[:, c * cw : (c + 1) * cw])

    spread(0)
    spread(1)
    spread(2)
    fold_core(0)
    spread(3)
    fold_core(1)
    fold_core(2)
    fold_z(0)
    fold_core(3)
    fold_z(1)
    fold_z(2)
    acc = mm_nt(d_pre[...], w_self[...])
    fold_z(3)
    for c in range(CHUNKS):
        acc += fold_y(c)

    h32 = mesh[...].astype(F32)
    scale = lax.rsqrt(jnp.mean(h32 * h32, axis=-1, keepdims=True) + 1e-05)
    normed = h32 * scale
    res_c[...] = (
        d_mesh[...] + scale * (acc - normed * jnp.mean(acc * normed, axis=-1, keepdims=True))
    ).astype(BF16)
    out_c = pltpu.make_async_copy(res_c, grad_mesh_hbm, store_sem.at[2])
    out_c.start()
    for copy in sends:
        copy.wait_send()
    out_a.wait()
    out_b.wait()
    out_c.wait()


def body(
    mesh_in,
    grid_in,
    cotangent,
    w_send,
    w_self,
    w_out,
    w_src,
    w_dst,
    w_dec,
    adj_blocks,
    adj_index,
    src_rows,
    dst_rows,
    counts,
):
    n = lax.axis_size("blk")
    per_dev, width = mesh_in.shape
    grid_rows = grid_in.shape[0]
    cw, ew = width // CHUNKS, width // EDGE_CHUNKS
    def vmem(*shape, dtype=BF16):
        return pltpu.VMEM(shape, dtype)

    dma = pltpu.SemaphoreType.DMA
    weight = vmem(width, width)
    pad = 384
    scratch = [
        vmem(per_dev, width),
        vmem(grid_rows, width),
        vmem(grid_rows, width),
        weight,
        weight,
        weight,
        weight,
        weight,
        weight,
        vmem(*adj_blocks.shape),
        pltpu.SMEM(adj_index.shape, jnp.int32),
        vmem(6, 8, 128, dtype=jnp.int32),
        vmem(per_dev, width),
        vmem(per_dev, width, dtype=F32),
        vmem(CHUNKS, 5, per_dev, cw),
        vmem(per_dev, 5 * per_dev),
        vmem(5 * per_dev, per_dev),
        vmem(5, 8, 128, dtype=jnp.int32),
        vmem(pad, per_dev),
        vmem(per_dev, pad),
        vmem(pad, 2 * grid_rows),
        vmem(grid_rows, pad),
        vmem(pad, width, dtype=F32),
        vmem(pad, width),
        vmem(per_dev, width),
        vmem(EDGE_CHUNKS, pad, ew),
        vmem(EDGE_CHUNKS, pad, ew),
        vmem(EDGE_CHUNKS, pad, ew),
        vmem(EDGE_CHUNKS, pad, ew),
        vmem(EDGE_CHUNKS, pad, ew),
        vmem(per_dev, width, dtype=F32),
        vmem(per_dev, width, dtype=F32),
        vmem(per_dev, width),
        vmem(CHUNKS, per_dev, cw, dtype=F32),
        vmem(CHUNKS, per_dev, cw, dtype=F32),
        vmem(CHUNKS, per_dev, cw, dtype=F32),
        vmem(CHUNKS, 2, per_dev, cw),
        vmem(CHUNKS, 2, per_dev, cw),
        vmem(CHUNKS, per_dev, cw),
        vmem(CHUNKS, per_dev, cw),
        vmem(CHUNKS, per_dev, cw),
        vmem(CHUNKS, per_dev, cw),
        vmem(grid_rows, width),
        vmem(grid_rows, width),
        vmem(per_dev, width),
        dma((11,)),
        dma((3,)),
        dma((5,)),
        dma((5,)),
        dma((CHUNKS, 4)),
        dma((CHUNKS, 4)),
        dma((EDGE_CHUNKS, 5)),
        dma((EDGE_CHUNKS, 5)),
        dma((EDGE_CHUNKS, 5)),
        dma((EDGE_CHUNKS, 5)),
        dma((CHUNKS, 2)),
        dma((CHUNKS, 2)),
        dma((CHUNKS,)),
        dma((CHUNKS,)),
        dma((CHUNKS,)),
        dma((CHUNKS,)),
    ]
    hbm = pl.BlockSpec(memory_space=pltpu.HBM)
    return pl.pallas_call(
        functools.partial(kernel, n),
        out_shape=(
            jax.ShapeDtypeStruct(grid_in.shape, BF16),
            jax.ShapeDtypeStruct(grid_in.shape, BF16),
            jax.ShapeDtypeStruct(mesh_in.shape, BF16),
        ),
        in_specs=[hbm] * 11 + [pl.BlockSpec(memory_space=pltpu.VMEM)] * 3,
        out_specs=(hbm, hbm, hbm),
        scratch_shapes=scratch,
        compiler_params=pltpu.CompilerParams(
            collective_id=0, has_side_effects=True, vmem_limit_bytes=64 * 1024 * 1024 - 65536
        ),
    )(
        mesh_in,
        grid_in,
        cotangent,
        w_send,
        w_self,
        w_out,
        w_src,
        w_dst,
        w_dec,
        adj_blocks,
        adj_index,
        src_rows,
        dst_rows,
        counts,
    )


def solution(mesh):
    rows = P(("groups", "blk"), None)
    return jax.shard_map(
        body,
        mesh=mesh,
        in_specs=(rows,) * 3
        + (P(),) * 6
        + (
            P("blk", None, None, None),
            P(),
            P("blk", None, None),
            P("blk", None, None),
            P("blk", None),
        ),
        out_specs=(rows, rows, rows),
        check_vma=False,
    )
```
